32 devices in a mesh: group: 4 (over y, x), member: 8 (over z, core).
Axes of the slice: x: 2, y: 2, z: 4, core: 2. Of those that a mesh axis runs over, the one named last changes fastest.
Arguments:
- entity_feats: bfloat16 [32768, 256], P(('group', 'member')), may hold values from -6 to 6
- grad_output: bfloat16 [32768, 256], P(('group', 'member')), may hold values from -6 to 6
- rel_table: bfloat16 [512, 256], replicated, may hold values from -5 to 5
- w_message: bfloat16 [256, 256], replicated, may hold values from -0.375 to 0.375
- w_qualifier: bfloat16 [256, 256], replicated, may hold values from -0.375 to 0.375
- mirror_rows: int32 [32, 64], P(('group', 'member')), may hold values from 0 to 1023
- subject_slot: int32 [65536], P(('group', 'member')), may hold values from 0 to 63
- object_slot: int32 [65536], P(('group', 'member')), may hold values from 0 to 63
- relation_ids: int32 [65536], P(('group', 'member')), may hold values from 0 to 511
- qual_relations: int32 [65536, 4], P(('group', 'member')), may hold values from 0 to 511
- qual_slots: int32 [65536, 4], P(('group', 'member')), may hold values from 0 to 63
- qual_mask: int32 [65536, 4], P(('group', 'member')), may hold values 0 or 1
- block_mask: int32 [512], P(('group', 'member')), may hold values 0 or 1
Outputs:
- grad_entities: float32 [32768, 256], P(('group', 'member'))
- grad_w_message: float32 [256, 256], replicated
- grad_w_qualifier: float32 [256, 256], replicated
The draws below stay inside these ranges and needn't reach their ends.
Inputs may be any that keep to these rules, and one draw needn't show every extreme that they name: `mirror_rows`: local entity rows of a master; rows may repeat, some rows are named by many devices. `subject_slot`: a mirror slot of the edge's own device. `object_slot`: a mirror slot of the edge's own device. `qual_slots`: a mirror slot of the edge's own device.
All inputs are finite; a program needn't handle non-finite values. No bound on the sum of `qual_mask` or of `block_mask` on one device may be relied on, other than what follows from the above.
Results may differ from the reference program's by a relative error of at most 0.0041.
Values may be sent and summed in bfloat16 or wider, within the bound.
A program may use at most 128 MiB of HBM per device.

```python
import math
import jax
import jax.numpy as jnp
import numpy as np
from jax import lax

D = 256
REL = 512
ENT_DEV = 1024
CAP = 2
BLOCKS_DEV = 16
QUAL = 4
EDGES_DEV = 2048
EDGES = 65536
BLOCKS = 512
ENTITIES = 32768
SLOTS = 64
DEVICES = 32


def touch_ends(array, rng, smallest, top_value):
    longest = array.shape.index(max(array.shape))
    spots = []
    for shift in (0, 1):
        where = [jax.random.randint(jax.random.fold_in(rng, axis), (), 0, length) for axis, length in enumerate(array.shape)]
        where[longest] = (where[longest] + shift) % array.shape[longest]
        spots.append(tuple(where))
    return array.at[spots[0]].set(smallest).at[spots[1]].set(top_value)


def steps_of(stream_key, extent, pieces, smallest, largest):
    def one(position, parts):
        draws = jax.random.uniform(jax.random.fold_in(jax.random.fold_in(stream_key, 6), position), (parts,), jnp.float32, smallest / len(pieces), largest / len(pieces))
        return jnp.repeat(jnp.exp(draws), extent[position] // parts).reshape((-1,) + (1,) * (len(extent) - position - 1))

    factor_of = one(*pieces[0])
    for cut in pieces[1:]:
        factor_of = factor_of * one(*cut)
    return factor_of


def rank_bounds(count, lean):
    weights = [(1 << 20) // math.isqrt(rank ** lean) + 1 for rank in range(1, count + 1)]
    deviation = 1 + sum(weights) // (1 << 30)
    return np.cumsum(np.array([max(1, weight // deviation) for weight in weights]))


def ranked(own_key, extent, amount, lean):
    grid = rank_bounds(amount, lean)
    lot = jax.random.randint(jax.random.fold_in(own_key, 1), extent, 0, int(grid[amount - 1]))
    grade = jnp.searchsorted(jnp.asarray(grid, jnp.int32), lot, side="right")
    return jax.random.permutation(jax.random.fold_in(own_key, 2), amount)[grade].astype(jnp.int32)


def bell_draw(rng, shape, spread, most, split=(), kind=jnp.bfloat16):
    loudness = steps_of(rng, shape, split, -0.22, 0.18) if split else 1.0
    drawn = jax.random.normal(rng, shape, jnp.float32) * spread * loudness
    return jnp.minimum(jnp.maximum(drawn, -most), most).astype(kind)


def setup_inputs(seed: int = 0) -> dict:
    key_list = jax.random.split(jax.random.key(seed), 14)
    entity_feats = bell_draw(key_list[0], (ENTITIES, D), 1.0, 6.0, ((0, 32),))
    grad_output = bell_draw(key_list[1], (ENTITIES, D), 1.0, 6.0, ((0, 32),))
    rel_table = bell_draw(key_list[2], (REL, D), 1.0, 5.0)
    w_message = bell_draw(key_list[3], (D, D), D ** -0.5, 0.375)
    w_qualifier = bell_draw(key_list[4], (D, D), D ** -0.5, 0.375)
    mirror_rows = touch_ends(ranked(key_list[5], (DEVICES, SLOTS), ENT_DEV, 2), jax.random.fold_in(key_list[5], 3), 0, ENT_DEV - 1).astype(jnp.int32)
    subject_slot = touch_ends(jax.random.randint(key_list[6], (EDGES,), 0, SLOTS), jax.random.fold_in(key_list[6], 1), 0, SLOTS - 1).astype(jnp.int32)
    object_slot = touch_ends(jax.random.randint(key_list[7], (EDGES,), 0, SLOTS), jax.random.fold_in(key_list[7], 1), 0, SLOTS - 1).astype(jnp.int32)
    relation_ids = touch_ends(jax.random.randint(key_list[8], (EDGES,), 0, REL), jax.random.fold_in(key_list[8], 1), 0, REL - 1).astype(jnp.int32)
    qual_relations = touch_ends(jax.random.randint(key_list[9], (EDGES, QUAL), 0, REL), jax.random.fold_in(key_list[9], 1), 0, REL - 1).astype(jnp.int32)
    qual_slots = touch_ends(jax.random.randint(key_list[10], (EDGES, QUAL), 0, SLOTS), jax.random.fold_in(key_list[10], 1), 0, SLOTS - 1).astype(jnp.int32)
    qual_mask = touch_ends((jax.random.randint(key_list[11], (EDGES, QUAL), 0, 3) < 2).astype(jnp.int32), jax.random.fold_in(key_list[11], 1), 0, 1)
    block_mask = touch_ends((jax.random.randint(key_list[12], (BLOCKS,), 0, 4) < 3).astype(jnp.int32), jax.random.fold_in(key_list[12], 1), 0, 1)
    return {"entity_feats": entity_feats, "grad_output": grad_output, "rel_table": rel_table, "w_message": w_message, "w_qualifier": w_qualifier, "mirror_rows": mirror_rows, "subject_slot": subject_slot, "object_slot": object_slot, "relation_ids": relation_ids, "qual_relations": qual_relations, "qual_slots": qual_slots, "qual_mask": qual_mask, "block_mask": block_mask}


def edge_work(mirror_x, mirror_g, rel_table, w_message, w_qualifier, subject_slot, object_slot, relation_ids, qual_relations, qual_slots, qual_mask, block_mask):
    slots = mirror_x.shape[0]
    width = mirror_x.shape[1]
    nblocks = block_mask.shape[0]
    edges = subject_slot.shape[0]
    live = jnp.broadcast_to(block_mask[:, None], (nblocks, edges // nblocks)).reshape(-1)
    x_subj = mirror_x[subject_slot]
    g_obj = mirror_g[object_slot] * live[:, None].astype(jnp.bfloat16)
    qual_x = mirror_x[qual_slots].astype(jnp.float32)
    qual_r = rel_table[qual_relations].astype(jnp.float32)
    qual_on = qual_mask.astype(jnp.float32)[:, :, None]
    qsum = jnp.sum(qual_on * qual_x * qual_r, axis=1).astype(jnp.bfloat16)
    qual_proj = jnp.dot(qsum, w_qualifier, preferred_element_type=jnp.float32)
    comp = 0.8 * rel_table[relation_ids].astype(jnp.float32) + 0.2 * qual_proj
    act = (x_subj.astype(jnp.float32) * comp).astype(jnp.bfloat16)
    dact = lax.dot_general(g_obj, w_message, (((1,), (1,)), ((), ())), preferred_element_type=jnp.float32)
    dsubj = dact * comp
    dqw = (0.2 * dact * x_subj.astype(jnp.float32)).astype(jnp.bfloat16)
    dq = lax.dot_general(dqw, w_qualifier, (((1,), (1,)), ((), ())), preferred_element_type=jnp.float32)
    dqual = qual_on * dq[:, None, :] * qual_r
    partials = jax.ops.segment_sum(dsubj, subject_slot, slots)
    partials = partials + jax.ops.segment_sum(dqual.reshape(-1, width), qual_slots.reshape(-1), slots)
    dw_msg = lax.dot_general(act, g_obj, (((0,), (0,)), ((), ())), preferred_element_type=jnp.float32)
    dw_qual = lax.dot_general(qsum, dqw, (((0,), (0,)), ((), ())), preferred_element_type=jnp.float32)
    return partials, dw_msg, dw_qual


def reference(entity_feats, grad_output, rel_table, w_message, w_qualifier, mirror_rows, subject_slot, object_slot, relation_ids, qual_relations, qual_slots, qual_mask, block_mask):
    masters = mirror_rows.reshape(DEVICES, DEVICES, CAP)
    masters = jnp.transpose(masters, (1, 0, 2))
    offsets = (jnp.arange(DEVICES, dtype=jnp.int32) * ENT_DEV).astype(jnp.int32)
    slot_entity = (masters + offsets[None, :, None]).reshape(DEVICES, SLOTS).astype(jnp.int32)

    def one_device(inputs):
        ids, subj, obj, rels, qrel, qslot, qmask, bmask = inputs
        return edge_work(entity_feats[ids], grad_output[ids], rel_table, w_message, w_qualifier, subj, obj, rels, qrel, qslot, qmask, bmask)

    partials, dw_msg, dw_qual = lax.map(one_device, (
        slot_entity,
        subject_slot.reshape(DEVICES, EDGES_DEV),
        object_slot.reshape(DEVICES, EDGES_DEV),
        relation_ids.reshape(DEVICES, EDGES_DEV),
        qual_relations.reshape(DEVICES, EDGES_DEV, QUAL),
        qual_slots.reshape(DEVICES, EDGES_DEV, QUAL),
        qual_mask.reshape(DEVICES, EDGES_DEV, QUAL),
        block_mask.reshape(DEVICES, BLOCKS_DEV)))
    grad_entities = jax.ops.segment_sum(partials.reshape(-1, D), slot_entity.reshape(-1), ENTITIES)
    scale = jnp.float32(EDGES) ** -0.5
    return grad_entities, scale * jnp.sum(dw_msg, axis=0), scale * jnp.sum(dw_qual, axis=0)
```

```python
import functools
import math

import jax
import jax.numpy as jnp
from jax import lax
from jax.experimental import pallas as pl
from jax.experimental.pallas import tpu as pltpu
from jax.sharding import PartitionSpec as P

F32 = jnp.float32
BF16 = jnp.bfloat16
MESH = pl.DeviceIdType.MESH
LANES = 128
TILE = 256
PAD = 8


def mm(a, b):
    return jnp.dot(a, b, preferred_element_type=F32)


def mm_nt(a, b):
    return lax.dot_general(a, b, (((1,), (1,)), ((), ())), preferred_element_type=F32)


def split(a):
    high = a.astype(BF16)
    return high, (a - high.astype(F32)).astype(BF16)


def onehot(row, depth):
    spots = lax.broadcasted_iota(jnp.int32, (depth, row.shape[1]), 0)
    return jnp.where(spots == row, 1.0, 0.0).astype(BF16)


def kernel(
    groups,
    members,
    reduce_here,
    feats,
    gout,
    rel,
    wm,
    wq,
    rows,
    subj,
    obj,
    rids,
    qrel,
    qslot,
    qmask,
    bmask,
    grad,
    dw,
    oh,
    oht,
    send_x,
    recv_x,
    send_p,
    recv_p,
    qr,
    rl,
    dqw_s,
    dsub_s,
    relt,
    wqt,
    mxt,
    mgt,
    qs,
    ob,
    part,
    acc,
    r1,
    c1,
    r2,
    own,
    c2,
    x_ss,
    x_rs,
    p_ss,
    p_rs,
    a_ss,
    a_rs,
    b_ss,
    b_rs,
    c_ss,
    c_rs,
    d_ss,
    d_rs,
):
    devices = groups * members
    g = lax.axis_index("group")
    m = lax.axis_index("member")
    me = g * members + m
    width = feats.shape[1]
    entities = feats.shape[0]
    slots = rows.shape[1]
    cap = slots // devices
    depth = mxt.shape[1]
    edges = subj.shape[1]
    quals = qrel.shape[0]
    nrel = rel.shape[0]
    nblocks = bmask.shape[1]
    tiles = edges // TILE
    block = edges // nblocks

    def peer(k):
        there = lax.rem(me + k, devices)
        return there, (there // members, lax.rem(there, members))

    barrier = pltpu.get_barrier_semaphore()

    def greet(k, _):
        pl.semaphore_signal(barrier, inc=1, device_id=peer(k)[1], device_id_type=MESH)
        return 0

    lax.fori_loop(1, devices, greet, 0)

    wide = devices * PAD
    k_of = lax.broadcasted_iota(jnp.int32, (wide, slots), 0)
    q_of = lax.broadcasted_iota(jnp.int32, (wide, slots), 1)
    wanted = (k_of // PAD) * cap + k_of % cap == q_of
    entry = jnp.sum(jnp.where(wanted, rows[...].astype(F32), 0.0), axis=1, keepdims=True)
    names = lax.broadcasted_iota(jnp.int32, (wide, entities), 1).astype(F32)
    picks = jnp.where(names == entry, 1.0, 0.0).astype(BF16)
    oh[...] = picks
    got = mm(picks, feats[...])
    gog = mm(picks, gout[...])
    part_of = lax.broadcasted_iota(jnp.int32, (wide, LANES), 0) % PAD // cap
    packed = jnp.where(
        part_of == 0,
        got[:, :LANES],
        jnp.where(
            part_of == 1,
            got[:, LANES:],
            jnp.where(part_of == 2, gog[:, :LANES], gog[:, LANES:]),
        ),
    )
    send_x[...] = packed.reshape(devices, PAD, LANES)

    pl.semaphore_wait(barrier, devices - 1)

    def x_copy(k):
        there, where = peer(k)
        return pltpu.make_async_remote_copy(
            src_ref=send_x.at[there],
            dst_ref=recv_x.at[me],
            send_sem=x_ss.at[k],
            recv_sem=x_rs.at[k],
            device_id=where,
            device_id_type=MESH,
        )

    def x_start(k, _):
        x_copy(k).start()
        return 0

    lax.fori_loop(1, devices, x_start, 0)
    recv_x[me] = send_x[me]

    relt[...] = rel[...].T
    wqt[...] = wq[...].T
    qs[...] = jnp.where(qmask[...] > 0, qslot[...], -1)
    for b in range(nblocks):
        at = pl.ds(b * block, block)
        ob[:, at] = jnp.where(bmask[:, b : b + 1] > 0, obj[:, at], -1)

    def look_up(t, _):
        at = pl.ds(pl.multiple_of(t * TILE, TILE), TILE)
        rl[:, at] = mm(relt[...], onehot(rids[:, at], nrel)).astype(BF16)
        for j in range(quals):
            qr[j, :, at] = mm(relt[...], onehot(qrel[j : j + 1, at], nrel)).astype(BF16)
        return 0

    lax.fori_loop(0, tiles, look_up, 0)

    def x_wait(k, _):
        x_copy(k).wait()
        return 0

    lax.fori_loop(1, devices, x_wait, 0)

    mirrors = recv_x[...].reshape(wide, LANES).astype(BF16)
    kk = lax.broadcasted_iota(jnp.int32, (wide, depth), 0)
    qq = lax.broadcasted_iota(jnp.int32, (wide, depth), 1)
    blocks = mirrors.T
    for part_no, ref in ((0, mxt), (1, mxt), (2, mgt), (3, mgt)):
        select = jnp.where(
            (kk == (qq // cap) * PAD + part_no * cap + qq % cap) & (qq < slots), 1.0, 0.0
        ).astype(BF16)
        half = (part_no % 2) * LANES
        ref[half : half + LANES, :] = mm(blocks, select).astype(BF16)

    acc[...] = jnp.zeros_like(acc)

    def first(t, _):
        at = pl.ds(pl.multiple_of(t * TILE, TILE), TILE)
        xs = mm(mxt[...], onehot(subj[:, at], depth))
        go = mm(mgt[...], onehot(ob[:, at], depth)).astype(BF16)
        total = None
        for j in range(quals):
            term = mm(mxt[...], onehot(qs[j : j + 1, at], depth)) * qr[j, :, at].astype(F32)
            total = term if total is None else total + term
        qsum = total.astype(BF16)
        comp = 0.8 * rl[:, at].astype(F32) + 0.2 * mm(wqt[...], qsum)
        act = (xs * comp).astype(BF16)
        dact = mm(wm[...], go)
        dsub_s[:, at] = (dact * comp).astype(BF16)
        dqw = (0.2 * dact * xs).astype(BF16)
        dqw_s[:, at] = dqw
        acc[:width, :] += mm_nt(act, go)
        acc[width:, :] += mm_nt(qsum, dqw)
        return 0

    lax.fori_loop(0, tiles, first, 0)

    scale = float(edges * devices) ** -0.5
    if reduce_here:
        acc[...] = acc[...] * scale
        big = acc.shape[0] // groups
        small = big // members

        def a_copy(k):
            there = lax.rem(g + k, groups)
            return pltpu.make_async_remote_copy(
                src_ref=acc.at[pl.ds(pl.multiple_of(there * big, big), big)],
                dst_ref=r1.at[k],
                send_sem=a_ss.at[k],
                recv_sem=a_rs.at[k],
                device_id=(there, m),
                device_id_type=MESH,
            )

        def b_copy(k):
            there = lax.rem(m + k, members)
            return pltpu.make_async_remote_copy(
                src_ref=c1.at[pl.ds(pl.multiple_of(there * small, small), small)],
                dst_ref=r2.at[k],
                send_sem=b_ss.at[k],
                recv_sem=b_rs.at[k],
                device_id=(g, there),
                device_id_type=MESH,
            )

        def c_copy(k):
            there = lax.rem(m + k, members)
            return pltpu.make_async_remote_copy(
                src_ref=own,
                dst_ref=c2.at[pl.ds(pl.multiple_of(m * small, small), small)],
                send_sem=c_ss.at[k],
                recv_sem=c_rs.at[k],
                device_id=(g, there),
                device_id_type=MESH,
            )

        def d_copy(k):
            there = lax.rem(g + k, groups)
            return pltpu.make_async_remote_copy(
                src_ref=c2,
                dst_ref=dw.at[pl.ds(pl.multiple_of(g * big, big), big)],
                send_sem=d_ss.at[k],
                recv_sem=d_rs.at[k],
                device_id=(there, m),
                device_id_type=MESH,
            )

        for k in range(1, groups):
            a_copy(k).start()

    part[...] = jnp.zeros_like(part)

    def second(t, _):
        at = pl.ds(pl.multiple_of(t * TILE, TILE), TILE)
        dq = mm(wq[...], dqw_s[:, at])
        total = mm_nt(onehot(subj[:, at], depth), dsub_s[:, at])
        for j in range(quals):
            dqual = (dq * qr[j, :, at].astype(F32)).astype(BF16)
            total += mm_nt(onehot(qs[j : j + 1, at], depth), dqual)
        part[...] += total
        return 0

    lax.fori_loop(0, tiles // 2, second, 0)

    if reduce_here:
        total = acc[pl.ds(pl.multiple_of(g * big, big), big), :]
        for k in range(1, groups):
            a_copy(k).wait()
            total = total + r1[k]
        c1[...] = total
        for k in range(1, members):
            b_copy(k).start()

    lax.fori_loop(tiles // 2, tiles, second, 0)

    kr = lax.broadcasted_iota(jnp.int32, (wide, depth), 0)
    qc = lax.broadcasted_iota(jnp.int32, (wide, depth), 1)
    pick = jnp.where((kr // PAD) * cap + kr % cap == qc, 1.0, 0.0).astype(BF16)
    high, low = split(part[...])
    outgoing = mm(pick, high) + mm(pick, low)
    send_p[...] = jnp.where(part_of == 0, outgoing[:, :LANES], outgoing[:, LANES:]).reshape(
        devices, PAD, LANES
    )

    def p_copy(k):
        there, where = peer(k)
        return pltpu.make_async_remote_copy(
            src_ref=send_p.at[there],
            dst_ref=recv_p.at[me],
            send_sem=p_ss.at[k],
            recv_sem=p_rs.at[k],
            device_id=where,
            device_id_type=MESH,
        )

    def p_start(k, _):
        p_copy(k).start()
        return 0

    lax.fori_loop(1, devices, p_start, 0)
    recv_p[me] = send_p[me]

    if reduce_here:
        total = c1[pl.ds(pl.multiple_of(m * small, small), small), :]
        for k in range(1, members):
            b_copy(k).wait()
            total = total + r2[k]
        own[...] = total
        for k in range(1, members):
            c_copy(k).start()
        c2[pl.ds(pl.multiple_of(m * small, small), small), :] = total

    oht[...] = oh[...].T

    if reduce_here:
        for k in range(1, members):
            c_copy(k).wait()
        for k in range(1, groups):
            d_copy(k).start()
        dw[pl.ds(pl.multiple_of(g * big, big), big), :] = c2[...]
    else:
        dw[...] = acc[...] * scale

    def p_wait(k, _):
        p_copy(k).wait()
        return 0

    lax.fori_loop(1, devices, p_wait, 0)
    back = recv_p[...].reshape(wide, LANES)
    for half in range(2):
        high, low = split(jnp.where(part_of == half, back, 0.0))
        grad[:, half * LANES : (half + 1) * LANES] = mm(oht[...], high) + mm(oht[...], low)

    if reduce_here:
        for k in range(1, groups):
            d_copy(k).wait()


def on_device(
    groups,
    members,
    entity_feats,
    grad_output,
    rel_table,
    w_message,
    w_qualifier,
    mirror_rows,
    subject_slot,
    object_slot,
    relation_ids,
    qual_relations,
    qual_slots,
    qual_mask,
    block_mask,
):
    devices = groups * members
    entities, width = entity_feats.shape
    slots = mirror_rows.shape[1]
    edges = subject_slot.shape[0]
    quals = qual_relations.shape[1]
    nrel = rel_table.shape[0]
    depth = max(slots, LANES)
    wide = devices * PAD
    total = 2 * width
    reduce_here = total % (groups * members * 16) == 0
    big = total // groups
    small = big // members if reduce_here else 16
    dma = pltpu.SemaphoreType.DMA
    grad, dw = pl.pallas_call(
        functools.partial(kernel, groups, members, reduce_here),
        out_shape=(
            jax.ShapeDtypeStruct((entities, width), F32),
            jax.ShapeDtypeStruct((total, width), F32),
        ),
        in_specs=[pl.BlockSpec(memory_space=pltpu.VMEM)] * 13,
        out_specs=[pl.BlockSpec(memory_space=pltpu.VMEM)] * 2,
        scratch_shapes=[
            pltpu.VMEM((wide, entities), BF16),
            pltpu.VMEM((entities, wide), BF16),
            pltpu.VMEM((devices, PAD, LANES), F32),
            pltpu.VMEM((devices, PAD, LANES), F32),
            pltpu.VMEM((devices, PAD, LANES), F32),
            pltpu.VMEM((devices, PAD, LANES), F32),
            pltpu.VMEM((quals, width, edges), BF16),
            pltpu.VMEM((width, edges), BF16),
            pltpu.VMEM((width, edges), BF16),
            pltpu.VMEM((width, edges), BF16),
            pltpu.VMEM((width, nrel), BF16),
            pltpu.VMEM((width, width), BF16),
            pltpu.VMEM((width, depth), BF16),
            pltpu.VMEM((width, depth), BF16),
            pltpu.VMEM((quals, edges), jnp.int32),
            pltpu.VMEM((1, edges), jnp.int32),
            pltpu.VMEM((depth, width), F32),
            pltpu.VMEM((total, width), F32),
            pltpu.VMEM((groups, big, width), F32),
            pltpu.VMEM((big, width), F32),
            pltpu.VMEM((members, small, width), F32),
            pltpu.VMEM((small, width), F32),
            pltpu.VMEM((big, width), F32),
            dma((devices,)),
            dma((devices,)),
            dma((devices,)),
            dma((devices,)),
            dma((groups,)),
            dma((groups,)),
            dma((members,)),
            dma((members,)),
            dma((members,)),
            dma((members,)),
            dma((groups,)),
            dma((groups,)),
        ],
        compiler_params=pltpu.CompilerParams(
            collective_id=0, has_side_effects=True, vmem_limit_bytes=48 * 1024 * 1024
        ),
        cost_estimate=pl.CostEstimate(
            flops=8_000_000_000, bytes_accessed=5_000_000, transcendentals=0
        ),
    )(
        entity_feats,
        grad_output,
        rel_table,
        w_message,
        w_qualifier,
        mirror_rows,
        subject_slot.reshape(1, edges),
        object_slot.reshape(1, edges),
        relation_ids.reshape(1, edges),
        qual_relations.T,
        qual_slots.T,
        qual_mask.T,
        block_mask.reshape(1, -1),
    )
    if not reduce_here:
        dw = lax.psum(dw, ("group", "member"))
    return grad, dw[:width], dw[width:]


def solution(mesh):
    groups, members = mesh.shape["group"], mesh.shape["member"]
    rows = P(("group", "member"), None)
    flat = P(("group", "member"))
    return jax.shard_map(
        functools.partial(on_device, groups, members),
        mesh=mesh,
        in_specs=(rows, rows, P(), P(), P(), rows, flat, flat, flat, rows, rows, rows, flat),
        out_specs=(rows, P(), P()),
        check_vma=False,
    )
```

```python
import functools
import math

import jax
import jax.numpy as jnp
from jax import lax
from jax.experimental import pallas as pl
from jax.experimental.pallas import tpu as pltpu
from jax.sharding import PartitionSpec as P

F32 = jnp.float32
BF16 = jnp.bfloat16
MESH = pl.DeviceIdType.MESH
LANES = 128
TILE = 512
PAD = 8


def mm(a, b):
    return jnp.dot(a, b, preferred_element_type=F32)


def mm_nt(a, b):
    return lax.dot_general(a, b, (((1,), (1,)), ((), ())), preferred_element_type=F32)


def split(a):
    high = a.astype(BF16)
    return high, (a - high.astype(F32)).astype(BF16)


def onehot(row, depth):
    spots = lax.broadcasted_iota(jnp.int32, (depth, row.shape[1]), 0)
    return jnp.where(spots == row, 1.0, 0.0).astype(BF16)


def kernel(
    groups,
    members,
    reduce_here,
    feats_h,
    gout_h,
    rel_h,
    wm_h,
    wq_h,
    rows_h,
    subj_h,
    obj_h,
    rids_h,
    qrel_h,
    qslot_h,
    qmask_h,
    bmask_h,
    grad,
    dw,
    oh,
    oht,
    send_x,
    recv_x,
    send_p,
    recv_p,
    qr,
    rl,
    dqw_s,
    dsub_s,
    relt,
    wqt,
    mxt,
    mgt,
    qs,
    ob,
    part,
    acc,
    r1,
    c1,
    cb,
    r2,
    own,
    c2,
    d2,
    x_ss,
    x_rs,
    p_ss,
    p_rs,
    a_ss,
    a_rs,
    b_ss,
    b_rs,
    c_ss,
    c_rs,
    d_ss,
    d_rs,
    feats,
    gout,
    rel,
    wm,
    wq,
    rows,
    subj,
    obj,
    rids,
    qrel,
    qslot,
    qmask,
    bmask,
    in_s,
):
    devices = groups * members
    g = lax.axis_index("group")
    m = lax.axis_index("member")
    me = g * members + m
    width = feats.shape[1]
    entities = feats.shape[0]
    slots = rows.shape[1]
    cap = slots // devices
    depth = mxt.shape[1]
    edges = subj.shape[1]
    quals = qrel.shape[0]
    nrel = rel.shape[0]
    nblocks = bmask.shape[1]
    tiles = edges // TILE
    block = edges // nblocks

    def peer(k):
        there = lax.rem(me + k, devices)
        return there, (there // members, lax.rem(there, members))

    sources = (rows_h, feats_h, gout_h, rel_h, rids_h, qrel_h, qslot_h, qmask_h)
    sources += (bmask_h, obj_h, subj_h, wm_h, wq_h)
    places = (rows, feats, gout, rel, rids, qrel, qslot, qmask, bmask, obj, subj, wm, wq)
    loads = [
        pltpu.make_async_copy(source, place, in_s.at[i])
        for i, (source, place) in enumerate(zip(sources, places))
    ]
    for load in loads:
        load.start()

    barrier = pltpu.get_barrier_semaphore()

    def greet(k, _):
        pl.semaphore_signal(barrier, inc=1, device_id=peer(k)[1], device_id_type=MESH)
        return 0

    lax.fori_loop(1, devices, greet, 0)

    for load in loads[:3]:
        load.wait()

    wide = devices * PAD
    k_of = lax.broadcasted_iota(jnp.int32, (wide, slots), 0)
    q_of = lax.broadcasted_iota(jnp.int32, (wide, slots), 1)
    wanted = (k_of // PAD) * cap + k_of % cap == q_of
    entry = jnp.sum(jnp.where(wanted, rows[...].astype(F32), 0.0), axis=1, keepdims=True)
    names = lax.broadcasted_iota(jnp.int32, (wide, entities), 1).astype(F32)
    picks = jnp.where(names == entry, 1.0, 0.0).astype(BF16)
    oh[...] = picks
    got = mm(picks, feats[...])
    gog = mm(picks, gout[...])
    part_of = lax.broadcasted_iota(jnp.int32, (wide, LANES), 0) % PAD // cap
    packed = jnp.where(
        part_of == 0,
        got[:, :LANES],
        jnp.where(
            part_of == 1,
            got[:, LANES:],
            jnp.where(part_of == 2, gog[:, :LANES], gog[:, LANES:]),
        ),
    )
    send_x[...] = packed.reshape(devices, PAD, LANES)

    pl.semaphore_wait(barrier, devices - 1)

    def x_copy(k):
        there, where = peer(k)
        return pltpu.make_async_remote_copy(
            src_ref=send_x.at[there],
            dst_ref=recv_x.at[me],
            send_sem=x_ss.at[k],
            recv_sem=x_rs.at[k],
            device_id=where,
            device_id_type=MESH,
        )

    def x_start(k, _):
        x_copy(k).start()
        return 0

    lax.fori_loop(1, devices, x_start, 0)
    recv_x[me] = send_x[me]

    for load in loads[3:]:
        load.wait()

    relt[...] = rel[...].T
    wqt[...] = wq[...].T
    qs[...] = jnp.where(qmask[...] > 0, qslot[...], -1)
    for b in range(nblocks):
        at = pl.ds(b * block, block)
        ob[:, at] = jnp.where(bmask[:, b : b + 1] > 0, obj[:, at], -1)

    def look_up(t, _):
        at = pl.ds(pl.multiple_of(t * TILE, TILE), TILE)
        rl[:, at] = mm(relt[...], onehot(rids[:, at], nrel)).astype(BF16)
        for j in range(quals):
            qr[j, :, at] = mm(relt[...], onehot(qrel[j : j + 1, at], nrel)).astype(BF16)
        return 0

    lax.fori_loop(0, tiles, look_up, 0)

    def x_wait(k, _):
        x_copy(k).wait()
        return 0

    lax.fori_loop(1, devices, x_wait, 0)

    mirrors = recv_x[...].reshape(wide, LANES).astype(BF16)
    kk = lax.broadcasted_iota(jnp.int32, (wide, depth), 0)
    qq = lax.broadcasted_iota(jnp.int32, (wide, depth), 1)
    blocks = mirrors.T
    for part_no, ref in ((0, mxt), (1, mxt), (2, mgt), (3, mgt)):
        select = jnp.where(
            (kk == (qq // cap) * PAD + part_no * cap + qq % cap) & (qq < slots), 1.0, 0.0
        ).astype(BF16)
        half = (part_no % 2) * LANES
        ref[half : half + LANES, :] = mm(blocks, select).astype(BF16)

    acc[...] = jnp.zeros_like(acc)

    def first(t, _):
        at = pl.ds(pl.multiple_of(t * TILE, TILE), TILE)
        xs = mm(mxt[...], onehot(subj[:, at], depth))
        go = mm(mgt[...], onehot(ob[:, at], depth)).astype(BF16)
        total = None
        for j in range(quals):
            term = mm(mxt[...], onehot(qs[j : j + 1, at], depth)) * qr[j, :, at].astype(F32)
            total = term if total is None else total + term
        qsum = total.astype(BF16)
        comp = 0.8 * rl[:, at].astype(F32) + 0.2 * mm(wqt[...], qsum)
        act = (xs * comp).astype(BF16)
        dact = mm(wm[...], go)
        dsub_s[:, at] = (dact * comp).astype(BF16)
        dqw = (0.2 * dact * xs).astype(BF16)
        dqw_s[:, at] = dqw
        acc[:width, :] += mm_nt(act, go)
        acc[width:, :] += mm_nt(qsum, dqw)
        return 0

    lax.fori_loop(0, tiles, first, 0)

    scale = float(edges * devices) ** -0.5
    if reduce_here:
        core, chips = lax.rem(m, 2), devices // 2
        chip = me // 2
        half = acc.shape[0] // 2
        small = half // chips
        other = m + 1 - 2 * core
        mine = pl.ds(pl.multiple_of(core * half, half), half)
        theirs = pl.ds(pl.multiple_of((1 - core) * half, half), half)
        piece = pl.ds(pl.multiple_of(chip * small, small), small)

        def far(k):
            there = lax.rem(chip + k, chips)
            device = there * 2 + core
            return there, (device // members, lax.rem(device, members))

        a_copy = pltpu.make_async_remote_copy(
            src_ref=acc.at[theirs],
            dst_ref=r1,
            send_sem=a_ss,
            recv_sem=a_rs,
            device_id=(g, other),
            device_id_type=MESH,
        )

        def b_copy(k):
            there, where = far(k)
            return pltpu.make_async_remote_copy(
                src_ref=cb.at[pl.ds(pl.multiple_of(there * small, small), small)],
                dst_ref=r2.at[k],
                send_sem=b_ss.at[k],
                recv_sem=b_rs.at[k],
                device_id=where,
                device_id_type=MESH,
            )

        def c_copy(k):
            return pltpu.make_async_remote_copy(
                src_ref=own,
                dst_ref=c2.at[piece],
                send_sem=c_ss.at[k],
                recv_sem=c_rs.at[k],
                device_id=far(k)[1],
                device_id_type=MESH,
            )

        d_copy = pltpu.make_async_remote_copy(
            src_ref=c2,
            dst_ref=d2,
            send_sem=d_ss,
            recv_sem=d_rs,
            device_id=(g, other),
            device_id_type=MESH,
        )

        def b_start(k, _):
            b_copy(k).start()
            return 0

        def b_wait(k, _):
            b_copy(k).wait()
            return 0

        def c_start(k, _):
            c_copy(k).start()
            return 0

        def c_wait(k, _):
            c_copy(k).wait()
            return 0

        a_copy.start()

    part[...] = jnp.zeros_like(part)

    def second(t, _):
        at = pl.ds(pl.multiple_of(t * TILE, TILE), TILE)
        dq = mm(wq[...], dqw_s[:, at])
        total = mm_nt(onehot(subj[:, at], depth), dsub_s[:, at])
        for j in range(quals):
            dqual = (dq * qr[j, :, at].astype(F32)).astype(BF16)
            total += mm_nt(onehot(qs[j : j + 1, at], depth), dqual)
        part[...] += total
        return 0

    lax.fori_loop(0, tiles // 4, second, 0)

    if reduce_here:
        a_copy.wait()
        c1[...] = (acc[mine, :] + r1[...]) * scale
        cb[...] = c1[...].astype(BF16)
        lax.fori_loop(1, chips, b_start, 0)

    lax.fori_loop(tiles // 4, tiles, second, 0)

    kr = lax.broadcasted_iota(jnp.int32, (wide, depth), 0)
    qc = lax.broadcasted_iota(jnp.int32, (wide, depth), 1)
    pick = jnp.where((kr // PAD) * cap + kr % cap == qc, 1.0, 0.0).astype(BF16)
    high, low = split(part[...])
    outgoing = mm(pick, high) + mm(pick, low)
    send_p[...] = jnp.where(part_of == 0, outgoing[:, :LANES], outgoing[:, LANES:]).reshape(
        devices, PAD, LANES
    )

    def p_copy(k):
        there, where = peer(k)
        return pltpu.make_async_remote_copy(
            src_ref=send_p.at[there, pl.ds(0, PAD // 2)],
            dst_ref=recv_p.at[me, pl.ds(0, PAD // 2)],
            send_sem=p_ss.at[k],
            recv_sem=p_rs.at[k],
            device_id=where,
            device_id_type=MESH,
        )

    def p_start(k, _):
        p_copy(k).start()
        return 0

    lax.fori_loop(1, devices, p_start, 0)
    recv_p[me] = send_p[me]

    if reduce_here:
        lax.fori_loop(1, chips, b_wait, 0)
        total = c1[piece, :]
        for k in range(1, chips):
            total = total + r2[k].astype(F32)
        own[...] = total.astype(BF16)
        lax.fori_loop(1, chips, c_start, 0)
        c2[piece, :] = own[...]
    else:
        dw[...] = acc[...] * scale

    oht[...] = oh[...].T

    def p_wait(k, _):
        p_copy(k).wait()
        return 0

    lax.fori_loop(1, devices, p_wait, 0)
    back = recv_p[...].reshape(wide, LANES)
    for half in range(2):
        high, low = split(jnp.where(part_of == half, back, 0.0))
        grad[:, half * LANES : (half + 1) * LANES] = mm(oht[...], high) + mm(oht[...], low)

    if reduce_here:
        lax.fori_loop(1, chips, c_wait, 0)
        d_copy.start()
        dw[mine, :] = c2[...].astype(F32)
        d_copy.wait()
        dw[theirs, :] = d2[...].astype(F32)


def on_device(
    groups,
    members,
    entity_feats,
    grad_output,
    rel_table,
    w_message,
    w_qualifier,
    mirror_rows,
    subject_slot,
    object_slot,
    relation_ids,
    qual_relations,
    qual_slots,
    qual_mask,
    block_mask,
):
    devices = groups * members
    entities, width = entity_feats.shape
    slots = mirror_rows.shape[1]
    edges = subject_slot.shape[0]
    quals = qual_relations.shape[1]
    nrel = rel_table.shape[0]
    depth = max(slots, LANES)
    wide = devices * PAD
    total = 2 * width
    chips = devices // 2
    reduce_here = members % 2 == 0 and total % (devices * 16) == 0
    half = total // 2
    small = half // chips if reduce_here else 16
    operands = (
        entity_feats,
        grad_output,
        rel_table,
        w_message,
        w_qualifier,
        mirror_rows,
        subject_slot.reshape(1, edges),
        object_slot.reshape(1, edges),
        relation_ids.reshape(1, edges),
        qual_relations.T,
        qual_slots.T,
        qual_mask.T,
        block_mask.reshape(1, -1),
    )
    dma = pltpu.SemaphoreType.DMA
    grad, dw = pl.pallas_call(
        functools.partial(kernel, groups, members, reduce_here),
        out_shape=(
            jax.ShapeDtypeStruct((entities, width), F32),
            jax.ShapeDtypeStruct((total, width), F32),
        ),
        in_specs=[pl.BlockSpec(memory_space=pltpu.HBM)] * 13,
        out_specs=[pl.BlockSpec(memory_space=pltpu.VMEM)] * 2,
        scratch_shapes=[
            pltpu.VMEM((wide, entities), BF16),
            pltpu.VMEM((entities, wide), BF16),
            pltpu.VMEM((devices, PAD, LANES), F32),
            pltpu.VMEM((devices, PAD, LANES), F32),
            pltpu.VMEM((devices, PAD, LANES), F32),
            pltpu.VMEM((devices, PAD, LANES), F32),
            pltpu.VMEM((quals, width, edges), BF16),
            pltpu.VMEM((width, edges), BF16),
            pltpu.VMEM((width, edges), BF16),
            pltpu.VMEM((width, edges), BF16),
            pltpu.VMEM((width, nrel), BF16),
            pltpu.VMEM((width, width), BF16),
            pltpu.VMEM((width, depth), BF16),
            pltpu.VMEM((width, depth), BF16),
            pltpu.VMEM((quals, edges), jnp.int32),
            pltpu.VMEM((1, edges), jnp.int32),
            pltpu.VMEM((depth, width), F32),
            pltpu.VMEM((total, width), F32),
            pltpu.VMEM((half, width), F32),
            pltpu.VMEM((half, width), F32),
            pltpu.VMEM((half, width), BF16),
            pltpu.VMEM((chips, small, width), BF16),
            pltpu.VMEM((small, width), BF16),
            pltpu.VMEM((half, width), BF16),
            pltpu.VMEM((half, width), BF16),
            dma((devices,)),
            dma((devices,)),
            dma((devices,)),
            dma((devices,)),
            dma,
            dma,
            dma((chips,)),
            dma((chips,)),
            dma((chips,)),
            dma((chips,)),
            dma,
            dma,
            *(pltpu.VMEM(a.shape, a.dtype) for a in operands),
            dma((len(operands),)),
        ],
        compiler_params=pltpu.CompilerParams(
            collective_id=0, has_side_effects=True, vmem_limit_bytes=63 * 1024 * 1024
        ),
        cost_estimate=pl.CostEstimate(
            flops=8_000_000_000, bytes_accessed=5_000_000, transcendentals=0
        ),
    )(*operands)
    if not reduce_here:
        dw = lax.psum(dw, ("group", "member"))
    return grad, dw[:width], dw[width:]


def solution(mesh):
    groups, members = mesh.shape["group"], mesh.shape["member"]
    rows = P(("group", "member"), None)
    flat = P(("group", "member"))
    return jax.shard_map(
        functools.partial(on_device, groups, members),
        mesh=mesh,
        in_specs=(rows, rows, P(), P(), P(), rows, flat, flat, flat, rows, rows, rows, flat),
        out_specs=(rows, P(), P()),
        check_vma=False,
    )
```
